32 devices in a mesh: groups: 2 (over y), tensor: 4 (over x, core), task: 4 (over z).
Axes of the slice: x: 2, y: 2, z: 4, core: 2. Of those that a mesh axis runs over, the one named last changes fastest.
Arguments:
- tokens: bfloat16 [3072, 8192], P(('groups', 'task'), 'tensor'), parts along dimension 0, may hold values from -6 to 6
- task_counts: int32 [512], P(('groups', 'task')), parts along dimension 0, may hold values from 0 to 96, as said below
- task_embeddings: bfloat16 [512, 1024], P(('groups', 'task')), parts along dimension 0, may hold values from -6 to 6
- embedding_weight: bfloat16 [1024, 512], replicated, may hold values from -0.1875 to 0.1875
- down_factor_head: bfloat16 [512, 16, 8192], P('task', None, 'tensor'), may hold values from -0.0029296875 to 0.0029296875
- query_up_head: bfloat16 [512, 8, 4096], P('task', None, 'tensor'), may hold values from -0.09375 to 0.09375
- value_up_head: bfloat16 [512, 8, 1024], P('task', None, 'tensor'), may hold values from -0.09375 to 0.09375
- w_query: bfloat16 [8192, 4096], P('tensor'), may hold values from -0.0625 to 0.0625
- w_value: bfloat16 [8192, 1024], P('tensor'), may hold values from -0.0625 to 0.0625
Outputs:
- query: bfloat16 [3072, 4096], P(('groups', 'task', 'tensor')), parts along dimension 0
- value: bfloat16 [3072, 1024], P(('groups', 'task', 'tensor')), parts along dimension 0
- down_factors: bfloat16 [512, 16, 8192], P(('groups', 'task'), None, 'tensor'), parts along dimension 0
- query_up_factors: bfloat16 [512, 8, 4096], P(('groups', 'task'), None, 'tensor'), parts along dimension 0
- value_up_factors: bfloat16 [512, 8, 1024], P(('groups', 'task'), None, 'tensor'), parts along dimension 0
The draws below stay inside these ranges and needn't reach their ends.
There are 2 independent parts, one for each index of `groups`. The reference program is written for one: setup_inputs(seed, part) draws one part's arguments, and reference() takes and returns one part's arrays. A program takes and returns all parts, laid end to end along the dimension named above; an argument that names none is the same for every part. Nothing has to cross between parts.
Inputs may be any that keep to these rules, and one draw needn't show every extreme that they name: For every k the task_counts of tasks k * 16 to k * 16 + 15 sum to at most 96; in every draw at least one task has exactly 96 tokens.
All inputs are finite; a program needn't handle non-finite values.
Results may differ from the reference program's by a relative error of at most 0.0059.
Values may be sent and summed in bfloat16 or wider, within the bound.
A program may use at most 128 MiB of HBM per device.

```python
import jax
import jax.numpy as jnp
from jax import lax

MODEL_WIDTH = 8192
VALUE_WIDTH = 1024
QUERY_FEATURES = 4096
ADAPTER_RANK = 8
E = 1024
H = 512
NTASK = 256
TOKENS = 1536
BLOCK_ROWS = 96
TASKS_PER_BLOCK = 16


def draw_task_counts(key, part):
    groups = NTASK // TASKS_PER_BLOCK
    keys = jax.random.split(key, 5)
    selected_factors = jax.random.randint(keys[0], (groups,), 0, TASKS_PER_BLOCK)
    marker = (jnp.arange(TASKS_PER_BLOCK)[None, :] == selected_factors[:, None]).astype(jnp.int32)
    served = jnp.maximum(jax.random.randint(keys[1], (groups, TASKS_PER_BLOCK), 0, 2), marker)
    full_group = jax.random.randint(keys[2], (), 0, groups)
    is_full = jnp.arange(groups) == full_group
    served = jnp.where(is_full[:, None], marker, served)
    weights = served * jax.random.randint(keys[3], (groups, TASKS_PER_BLOCK), 1, 9)
    lowest = max(1, BLOCK_ROWS // 8)
    totals = jax.random.randint(keys[4], (groups,), lowest, BLOCK_ROWS + 1)
    totals = jnp.where(is_full, BLOCK_ROWS, totals)
    shares = totals[:, None] * weights // jnp.sum(weights, axis=1, keepdims=True)
    shares = shares + marker * (totals - jnp.sum(shares, axis=1))[:, None]
    return shares.reshape(NTASK).astype(jnp.int32)


def block_scale(rng, extent, cuts, least, largest):
    loudness = 1.0
    for dim, blocks in cuts:
        draws = jax.random.uniform(jax.random.fold_in(jax.random.fold_in(rng, 6), dim), (blocks,), jnp.float32, least / len(cuts), largest / len(cuts))
        loudness = loudness * jnp.repeat(jnp.exp(draws), extent[dim] // blocks).reshape((-1,) + (1,) * (len(extent) - 1 - dim))
    return loudness


def centred(rng, extent, deviation, most, cuts=(), kind=jnp.bfloat16):
    array = jax.random.normal(rng, extent, jnp.float32) * deviation
    if len(cuts) > 0:
        array = block_scale(rng, extent, cuts, -0.22, 0.18) * array
    return jnp.clip(array, min=-most, max=most).astype(kind)


def setup_inputs(seed: int = 0, part: int = 0) -> dict:
    splits = jax.random.split(jax.random.key(seed), 10)
    own_keys = jax.random.split(jax.random.fold_in(splits[9], part), 10)
    tokens = centred(own_keys[0], (TOKENS, MODEL_WIDTH), 1.0, 6.0, ((0, 4), (1, 4)))
    task_counts = draw_task_counts(jax.random.fold_in(jax.random.fold_in(splits[9], part), 71), part)
    task_embeddings = centred(own_keys[2], (NTASK, E), 1.0, 6.0, ((0, 4),))
    embedding_weight = centred(splits[3], (E, H), E ** -0.5, 0.1875)
    down_factor_head = centred(splits[4], (H, 2 * ADAPTER_RANK, MODEL_WIDTH), (H * MODEL_WIDTH) ** -0.5, 0.0029296875, ((0, 4), (2, 4)))
    query_up_head = centred(splits[5], (H, ADAPTER_RANK, QUERY_FEATURES), (H * ADAPTER_RANK) ** -0.5, 0.09375, ((0, 4), (2, 4)))
    value_up_head = centred(splits[6], (H, ADAPTER_RANK, VALUE_WIDTH), (H * ADAPTER_RANK) ** -0.5, 0.09375, ((0, 4), (2, 4)))
    w_query = centred(splits[7], (MODEL_WIDTH, QUERY_FEATURES), MODEL_WIDTH ** -0.5, 0.0625, ((0, 4),))
    w_value = centred(splits[8], (MODEL_WIDTH, VALUE_WIDTH), MODEL_WIDTH ** -0.5, 0.0625, ((0, 4),))
    return dict(tokens=tokens, task_counts=task_counts, task_embeddings=task_embeddings, embedding_weight=embedding_weight, down_factor_head=down_factor_head, query_up_head=query_up_head, value_up_head=value_up_head, w_query=w_query, w_value=w_value)


ADAPTER_SCALE = 2.0


def produce_head(hypernet_hidden, matrix):
    flattened = jnp.dot(hypernet_hidden, matrix.reshape(matrix.shape[0], -1), preferred_element_type=jnp.float32)
    return flattened.astype(jnp.bfloat16).reshape(hypernet_hidden.shape[0], matrix.shape[1], matrix.shape[2])


def reference(tokens, task_counts, task_embeddings, embedding_weight, down_factor_head, query_up_head, value_up_head, w_query, w_value):
    hypernet_hidden = jax.nn.silu(jnp.dot(task_embeddings, embedding_weight, preferred_element_type=jnp.float32)).astype(jnp.bfloat16)
    down_factors = produce_head(hypernet_hidden, down_factor_head)
    query_up_factors = produce_head(hypernet_hidden, query_up_head)
    value_up_factors = produce_head(hypernet_hidden, value_up_head)
    token_blocks = TOKENS // BLOCK_ROWS
    tallies = task_counts.reshape(token_blocks, TASKS_PER_BLOCK)
    finish = jnp.cumsum(tallies, axis=1)
    starts = finish - tallies
    positions = jnp.arange(BLOCK_ROWS, dtype=jnp.int32)
    member = ((positions[None, :, None] >= starts[:, None, :]) & (positions[None, :, None] < finish[:, None, :])).astype(jnp.float32)
    base_product = jnp.concatenate((jnp.dot(tokens, w_query, preferred_element_type=jnp.float32), jnp.dot(tokens, w_value, preferred_element_type=jnp.float32)), axis=1)
    stretches = tokens.reshape(token_blocks, BLOCK_ROWS, MODEL_WIDTH).astype(jnp.float32)
    task_adapters = down_factors.reshape(token_blocks, TASKS_PER_BLOCK, 2 * ADAPTER_RANK, MODEL_WIDTH).astype(jnp.float32)
    projected = jnp.einsum("bpd,bmrd->bpmr", stretches, task_adapters, precision=lax.Precision.HIGHEST)
    selected_factors = projected * member[..., None]
    query_up_factor = query_up_factors.reshape(token_blocks, TASKS_PER_BLOCK, ADAPTER_RANK, QUERY_FEATURES).astype(jnp.float32)
    value_up_factor = value_up_factors.reshape(token_blocks, TASKS_PER_BLOCK, ADAPTER_RANK, VALUE_WIDTH).astype(jnp.float32)
    delta_query = jnp.einsum("osxe,oxea->osa", selected_factors[..., :ADAPTER_RANK], query_up_factor, precision=lax.Precision.HIGHEST)
    delta_value = jnp.einsum("osxe,oxea->osa", selected_factors[..., ADAPTER_RANK:], value_up_factor, precision=lax.Precision.HIGHEST)
    adapter_update = jnp.concatenate((delta_query, delta_value), axis=2).reshape(TOKENS, QUERY_FEATURES + VALUE_WIDTH)
    combined_output = base_product + ADAPTER_SCALE * adapter_update
    return (combined_output[:, :QUERY_FEATURES].astype(jnp.bfloat16), combined_output[:, QUERY_FEATURES:].astype(jnp.bfloat16), down_factors, query_up_factors, value_up_factors)
```

```python
import jax
import jax.numpy as jnp
from jax import lax
from jax.sharding import PartitionSpec as P

ADAPTER_SCALE = 2.0


def block_member(counts, blocks, block_tasks, block_rows):
    tallies = counts.reshape(blocks, block_tasks)
    order = jnp.arange(block_tasks, dtype=jnp.int32)
    upto = order[None, :, None] >= order[None, None, :]
    finish = jnp.sum(jnp.where(upto, tallies[:, None, :], 0), axis=2)
    starts = finish - tallies
    positions = jnp.arange(block_rows, dtype=jnp.int32)
    inside = (positions[None, :, None] >= starts[:, None, :]) & (
        positions[None, :, None] < finish[:, None, :]
    )
    return inside.astype(jnp.float32)


def pack_head(head, n_groups, n_task):
    units, ranks, width = head.shape
    own = width // n_groups
    part = lax.dynamic_slice_in_dim(head, lax.axis_index("groups") * own, own, axis=2)
    part = part.reshape(units, ranks, n_task, own // n_task)
    return part.transpose(2, 0, 1, 3).reshape(n_task, units, -1)


def regroup(packed):
    got = lax.all_to_all(packed, "task", split_axis=0, concat_axis=0, tiled=True)
    return got.reshape(-1, got.shape[2])


def emit(every_hidden, matrix, n_owners):
    made = jnp.dot(every_hidden, matrix, preferred_element_type=jnp.float32)
    made = made.astype(jnp.bfloat16).reshape(n_owners, -1, matrix.shape[1])
    return lax.all_to_all(
        made, ("groups", "task"), split_axis=0, concat_axis=0, tiled=True
    )


def unpack_factor(got, ranks):
    owners, tasks, flat = got.shape
    return (
        got.reshape(owners, tasks, ranks, flat // ranks)
        .transpose(1, 2, 0, 3)
        .reshape(tasks, ranks, -1)
    )


def local(
    tokens,
    task_counts,
    task_embeddings,
    embedding_weight,
    down_factor_head,
    query_up_head,
    value_up_head,
    w_query,
    w_value,
):
    n_groups, n_task = lax.axis_size("groups"), lax.axis_size("task")
    n_owners = n_groups * n_task
    blocks = lax.axis_size("tensor")
    rank = query_up_head.shape[1]
    rows, shard_width = tokens.shape
    block_rows = rows // blocks
    block_tasks = task_counts.shape[0] // blocks

    low, high = down_factor_head[:, :rank], down_factor_head[:, rank:]
    down0 = regroup(pack_head(low, n_groups, n_task))
    down1 = regroup(pack_head(high, n_groups, n_task))
    packed_query = pack_head(query_up_head, n_groups, n_task)
    packed_value = pack_head(value_up_head, n_groups, n_task)
    up = regroup(jnp.concatenate((packed_query, packed_value), axis=2))

    hidden = jax.nn.silu(
        jnp.dot(task_embeddings, embedding_weight, preferred_element_type=jnp.float32)
    ).astype(jnp.bfloat16)
    every_hidden = lax.all_gather(hidden, ("groups", "task"), axis=0, tiled=True)

    base_query = lax.psum_scatter(
        jnp.dot(tokens, w_query, preferred_element_type=jnp.float32),
        "tensor", scatter_dimension=0, tiled=True,
    )
    base_value = lax.psum_scatter(
        jnp.dot(tokens, w_value, preferred_element_type=jnp.float32),
        "tensor", scatter_dimension=0, tiled=True,
    )

    half0 = unpack_factor(emit(every_hidden, down0, n_owners), rank)
    half1 = unpack_factor(emit(every_hidden, down1, n_owners), rank)
    got_up = emit(every_hidden, up, n_owners)
    flat_query = packed_query.shape[2]
    query_up_factors = unpack_factor(got_up[:, :, :flat_query], rank)
    value_up_factors = unpack_factor(got_up[:, :, flat_query:], rank)
    down_factors = jnp.concatenate((half0, half1), axis=1)

    member = block_member(task_counts, blocks, block_tasks, block_rows)
    stretches = tokens.reshape(blocks, block_rows, shard_width)

    def project(half):
        made = jnp.einsum(
            "bpd,bmrd->bpmr",
            stretches,
            half.reshape(blocks, block_tasks, rank, shard_width),
            preferred_element_type=jnp.float32,
        )
        return jnp.sum(made * member[..., None], axis=2).reshape(rows, rank)

    low_rank = lax.psum_scatter(
        jnp.concatenate((project(half0), project(half1)), axis=1),
        "tensor", scatter_dimension=0, tiled=True,
    )
    own_member = lax.dynamic_index_in_dim(
        member, lax.axis_index("tensor"), axis=0, keepdims=False
    )

    def delta(part, factors):
        spread = (own_member[:, :, None] * part[:, None, :]).reshape(block_rows, -1)
        whole = lax.all_to_all(factors, "tensor", split_axis=0, concat_axis=2, tiled=True)
        return jnp.dot(
            spread,
            whole.reshape(block_tasks * rank, -1).astype(jnp.float32),
            precision=lax.Precision.HIGHEST,
        )

    query = base_query + ADAPTER_SCALE * delta(low_rank[:, :rank], query_up_factors)
    value = base_value + ADAPTER_SCALE * delta(low_rank[:, rank:], value_up_factors)
    return (
        query.astype(jnp.bfloat16),
        value.astype(jnp.bfloat16),
        down_factors,
        query_up_factors,
        value_up_factors,
    )


def solution(mesh):
    return jax.shard_map(
        local,
        mesh=mesh,
        in_specs=(
            P(("groups", "task"), "tensor"),
            P(("groups", "task")),
            P(("groups", "task"), None),
            P(),
            P("task", None, "tensor"),
            P("task", None, "tensor"),
            P("task", None, "tensor"),
            P("tensor", None),
            P("tensor", None),
        ),
        out_specs=(
            P(("groups", "task", "tensor"), None),
            P(("groups", "task", "tensor"), None),
            P(("groups", "task"), None, "tensor"),
            P(("groups", "task"), None, "tensor"),
            P(("groups", "task"), None, "tensor"),
        ),
        check_vma=False,
    )
```

```python
import jax
import jax.numpy as jnp
from jax import lax
from jax.sharding import PartitionSpec as P

ADAPTER_SCALE = 2.0


def block_member(counts, blocks, block_tasks, block_rows):
    tallies = counts.reshape(blocks, block_tasks)
    order = jnp.arange(block_tasks, dtype=jnp.int32)
    upto = order[None, :, None] >= order[None, None, :]
    finish = jnp.sum(jnp.where(upto, tallies[:, None, :], 0), axis=2)
    starts = finish - tallies
    positions = jnp.arange(block_rows, dtype=jnp.int32)
    inside = (positions[None, :, None] >= starts[:, None, :]) & (
        positions[None, :, None] < finish[:, None, :]
    )
    return inside.astype(jnp.float32)


def pack_head(head, n_groups, n_task):
    units, ranks, width = head.shape
    own = width // n_groups
    part = lax.dynamic_slice_in_dim(head, lax.axis_index("groups") * own, own, axis=2)
    part = part.reshape(units, ranks, n_task, own // n_task)
    return part.transpose(2, 0, 1, 3).reshape(n_task, units, -1)


def regroup(packed):
    got = lax.all_to_all(packed, "task", split_axis=0, concat_axis=0, tiled=True)
    return got.reshape(-1, got.shape[2])


def produce(every_hidden, matrix, n_owners):
    made = jnp.dot(every_hidden, matrix, preferred_element_type=jnp.float32)
    return made.astype(jnp.bfloat16).reshape(n_owners, -1, matrix.shape[1])


def to_owners(made):
    return lax.all_to_all(
        made, ("groups", "task"), split_axis=0, concat_axis=0, tiled=True
    )


def unpack_factor(got, ranks):
    owners, tasks, flat = got.shape
    return (
        got.reshape(owners, tasks, ranks, flat // ranks)
        .transpose(1, 2, 0, 3)
        .reshape(tasks, ranks, -1)
    )


def local(
    tokens,
    task_counts,
    task_embeddings,
    embedding_weight,
    down_factor_head,
    query_up_head,
    value_up_head,
    w_query,
    w_value,
):
    n_groups, n_task = lax.axis_size("groups"), lax.axis_size("task")
    n_owners = n_groups * n_task
    blocks = lax.axis_size("tensor")
    rank = query_up_head.shape[1]
    rows, shard_width = tokens.shape
    block_rows = rows // blocks
    block_tasks = task_counts.shape[0] // blocks

    after = lax.optimization_barrier

    packed_query = pack_head(query_up_head, n_groups, n_task)
    packed_value = pack_head(value_up_head, n_groups, n_task)
    packed_up = jnp.concatenate((packed_query, packed_value), axis=2)
    flat_query = packed_query.shape[2]
    up = regroup(packed_up)

    hidden = jax.nn.silu(
        jnp.dot(task_embeddings, embedding_weight, preferred_element_type=jnp.float32)
    ).astype(jnp.bfloat16)
    every_hidden = lax.all_gather(hidden, ("groups", "task"), axis=0, tiled=True)

    packed0 = pack_head(down_factor_head[:, :rank], n_groups, n_task)
    packed0, up, every_hidden = after((packed0, up, every_hidden))
    down0 = regroup(packed0)

    sums_query = jnp.dot(tokens, w_query, preferred_element_type=jnp.float32)
    sums_value = jnp.dot(tokens, w_value, preferred_element_type=jnp.float32)
    packed1 = pack_head(down_factor_head[:, rank:], n_groups, n_task)
    made_up = produce(every_hidden, up, n_owners)
    packed1, down0, sums_query, sums_value, made_up = after(
        (packed1, down0, sums_query, sums_value, made_up)
    )
    base_query = lax.psum_scatter(sums_query, "tensor", scatter_dimension=0, tiled=True)
    base_value = lax.psum_scatter(sums_value, "tensor", scatter_dimension=0, tiled=True)
    down1 = regroup(packed1)

    made0 = produce(every_hidden, down0, n_owners)
    made_up, made0, down1 = after((made_up, made0, down1))
    got_up = to_owners(made_up)
    made1 = produce(every_hidden, down1, n_owners)
    made0, made1, got_up = after((made0, made1, got_up))
    every_up = lax.all_gather(got_up, "tensor", axis=0, tiled=False)
    got0 = to_owners(made0)
    query_up_factors = unpack_factor(got_up[:, :, :flat_query], rank)
    value_up_factors = unpack_factor(got_up[:, :, flat_query:], rank)
    made1, got0, base_query, base_value, query_up_factors, value_up_factors = after(
        (made1, got0, base_query, base_value, query_up_factors, value_up_factors)
    )
    got1 = to_owners(made1)
    half0 = unpack_factor(got0, rank)
    half1 = unpack_factor(got1, rank)
    down_factors = jnp.concatenate((half0, half1), axis=1)

    member = block_member(task_counts, blocks, block_tasks, block_rows)
    stretches = tokens.reshape(blocks, block_rows, shard_width)

    def project(half):
        made = jnp.einsum(
            "bpd,bmrd->bpmr",
            stretches,
            half.reshape(blocks, block_tasks, rank, shard_width),
            preferred_element_type=jnp.float32,
        )
        return jnp.sum(made * member[..., None], axis=2).reshape(rows, rank)

    low_rank = lax.psum_scatter(
        jnp.concatenate((project(half0), project(half1)), axis=1),
        "tensor", scatter_dimension=0, tiled=True,
    )
    own_member = lax.dynamic_index_in_dim(
        member, lax.axis_index("tensor"), axis=0, keepdims=False
    )

    own_up = lax.dynamic_slice_in_dim(
        every_up, lax.axis_index("tensor") * block_tasks, block_tasks, axis=2
    )

    def delta(part, factors):
        spread = (own_member[:, :, None] * part[:, None, :]).reshape(block_rows, -1)
        columns = factors.shape[3] // rank
        whole = factors.reshape(-1, block_tasks, rank, columns).transpose(1, 2, 0, 3)
        return jnp.dot(
            spread,
            whole.reshape(block_tasks * rank, -1).astype(jnp.float32),
            precision=lax.Precision.HIGHEST,
        )

    query = base_query + ADAPTER_SCALE * delta(
        low_rank[:, :rank], own_up[..., :flat_query]
    )
    value = base_value + ADAPTER_SCALE * delta(
        low_rank[:, rank:], own_up[..., flat_query:]
    )
    return (
        query.astype(jnp.bfloat16),
        value.astype(jnp.bfloat16),
        down_factors,
        query_up_factors,
        value_up_factors,
    )


def solution(mesh):
    return jax.shard_map(
        local,
        mesh=mesh,
        in_specs=(
            P(("groups", "task"), "tensor"),
            P(("groups", "task")),
            P(("groups", "task"), None),
            P(),
            P("task", None, "tensor"),
            P("task", None, "tensor"),
            P("task", None, "tensor"),
            P("tensor", None),
            P("tensor", None),
        ),
        out_specs=(
            P(("groups", "task", "tensor"), None),
            P(("groups", "task", "tensor"), None),
            P(("groups", "task"), None, "tensor"),
            P(("groups", "task"), None, "tensor"),
            P(("groups", "task"), None, "tensor"),
        ),
        check_vma=False,
    )
```

```python
import jax
import jax.numpy as jnp
from jax import lax
from jax.sharding import PartitionSpec as P

ADAPTER_SCALE = 2.0


def block_member(counts, blocks, block_tasks, block_rows):
    tallies = counts.reshape(blocks, block_tasks)
    order = jnp.arange(block_tasks, dtype=jnp.int32)
    upto = order[None, :, None] >= order[None, None, :]
    finish = jnp.sum(jnp.where(upto, tallies[:, None, :], 0), axis=2)
    starts = finish - tallies
    positions = jnp.arange(block_rows, dtype=jnp.int32)
    inside = (positions[None, :, None] >= starts[:, None, :]) & (
        positions[None, :, None] < finish[:, None, :]
    )
    return inside.astype(jnp.float32)


def pack_head(head, n_groups, n_task):
    units, ranks, width = head.shape
    own = width // n_groups
    part = lax.dynamic_slice_in_dim(head, lax.axis_index("groups") * own, own, axis=2)
    part = part.reshape(units, ranks, n_task, own // n_task)
    return part.transpose(2, 0, 1, 3).reshape(n_task, units, -1)


def regroup(packed):
    got = lax.all_to_all(packed, "task", split_axis=0, concat_axis=0, tiled=True)
    return got.reshape(-1, got.shape[2])


def produce(every_hidden, matrix, n_owners):
    made = jnp.dot(every_hidden, matrix, preferred_element_type=jnp.float32)
    return made.astype(jnp.bfloat16).reshape(n_owners, -1, matrix.shape[1])


def to_owners(made):
    return lax.all_to_all(
        made, ("groups", "task"), split_axis=0, concat_axis=0, tiled=True
    )


def corner(array):
    return lax.slice(array, (0,) * array.ndim, (1,) * array.ndim)


def unpack_factor(got, ranks):
    owners, tasks, flat = got.shape
    return (
        got.reshape(owners, tasks, ranks, flat // ranks)
        .transpose(1, 2, 0, 3)
        .reshape(tasks, ranks, -1)
    )


def local(
    tokens,
    task_counts,
    task_embeddings,
    embedding_weight,
    down_factor_head,
    query_up_head,
    value_up_head,
    w_query,
    w_value,
):
    n_groups, n_task = lax.axis_size("groups"), lax.axis_size("task")
    n_owners = n_groups * n_task
    blocks = lax.axis_size("tensor")
    rank = query_up_head.shape[1]
    rows, shard_width = tokens.shape
    block_rows = rows // blocks
    block_tasks = task_counts.shape[0] // blocks

    after = lax.optimization_barrier

    packed_query = pack_head(query_up_head, n_groups, n_task)
    packed_value = pack_head(value_up_head, n_groups, n_task)
    packed_up = jnp.concatenate((packed_query, packed_value), axis=2)
    flat_query = packed_query.shape[2]

    hidden = jax.nn.silu(
        jnp.dot(task_embeddings, embedding_weight, preferred_element_type=jnp.float32)
    ).astype(jnp.bfloat16)
    every_hidden = to_owners(jnp.broadcast_to(hidden, (n_owners, *hidden.shape)))
    packed_up, _ = after((packed_up, corner(every_hidden)))
    every_hidden = every_hidden.reshape(-1, hidden.shape[1])
    up = regroup(packed_up)

    packed0 = pack_head(down_factor_head[:, :rank], n_groups, n_task)
    packed0, every_hidden, up = after((packed0, every_hidden, up))
    down0 = regroup(packed0)

    sums_query = jnp.dot(tokens, w_query, preferred_element_type=jnp.float32)
    sums_value = jnp.dot(tokens, w_value, preferred_element_type=jnp.float32)
    packed1 = pack_head(down_factor_head[:, rank:], n_groups, n_task)
    made_up = produce(every_hidden, up, n_owners)
    packed1, down0, sums_query, sums_value, made_up = after(
        (packed1, down0, sums_query, sums_value, made_up)
    )
    base_query = lax.psum_scatter(sums_query, "tensor", scatter_dimension=0, tiled=True)
    base_value = lax.psum_scatter(sums_value, "tensor", scatter_dimension=0, tiled=True)
    down1 = regroup(packed1)

    made0 = produce(every_hidden, down0, n_owners)
    made_up, made0, _ = after((made_up, made0, corner(down1)))
    got_up = to_owners(made_up)
    made1 = produce(every_hidden, down1, n_owners)
    made0, made1, got_up = after((made0, made1, got_up))
    every_up = lax.all_gather(got_up, "tensor", axis=0, tiled=False)
    got0 = to_owners(made0)
    query_up_factors = unpack_factor(got_up[:, :, :flat_query], rank)
    value_up_factors = unpack_factor(got_up[:, :, flat_query:], rank)
    made1, got0, base_query, base_value, query_up_factors, value_up_factors = after(
        (made1, got0, base_query, base_value, query_up_factors, value_up_factors)
    )
    got1 = to_owners(made1)
    half0 = unpack_factor(got0, rank)
    half1 = unpack_factor(got1, rank)
    down_factors = jnp.concatenate((half0, half1), axis=1)

    member = block_member(task_counts, blocks, block_tasks, block_rows)
    stretches = tokens.reshape(blocks, block_rows, shard_width)

    def project(half):
        made = jnp.einsum(
            "bpd,bmrd->bpmr",
            stretches,
            half.reshape(blocks, block_tasks, rank, shard_width),
            preferred_element_type=jnp.float32,
        )
        return jnp.sum(made * member[..., None], axis=2).reshape(rows, rank)

    low_rank = lax.psum_scatter(
        jnp.concatenate((project(half0), project(half1)), axis=1),
        "tensor", scatter_dimension=0, tiled=True,
    )
    own_member = lax.dynamic_index_in_dim(
        member, lax.axis_index("tensor"), axis=0, keepdims=False
    )

    own_up = lax.dynamic_slice_in_dim(
        every_up, lax.axis_index("tensor") * block_tasks, block_tasks, axis=2
    )

    def delta(part, factors):
        spread = (own_member[:, :, None] * part[:, None, :]).reshape(block_rows, -1)
        columns = factors.shape[3] // rank
        whole = factors.reshape(-1, block_tasks, rank, columns).transpose(1, 2, 0, 3)
        return jnp.dot(
            spread,
            whole.reshape(block_tasks * rank, -1).astype(jnp.float32),
            precision=lax.Precision.HIGHEST,
        )

    query = base_query + ADAPTER_SCALE * delta(
        low_rank[:, :rank], own_up[..., :flat_query]
    )
    value = base_value + ADAPTER_SCALE * delta(
        low_rank[:, rank:], own_up[..., flat_query:]
    )
    return (
        query.astype(jnp.bfloat16),
        value.astype(jnp.bfloat16),
        down_factors,
        query_up_factors,
        value_up_factors,
    )


def solution(mesh):
    return jax.shard_map(
        local,
        mesh=mesh,
        in_specs=(
            P(("groups", "task"), "tensor"),
            P(("groups", "task")),
            P(("groups", "task"), None),
            P(),
            P("task", None, "tensor"),
            P("task", None, "tensor"),
            P("task", None, "tensor"),
            P("tensor", None),
            P("tensor", None),
        ),
        out_specs=(
            P(("groups", "task", "tensor"), None),
            P(("groups", "task", "tensor"), None),
            P(("groups", "task"), None, "tensor"),
            P(("groups", "task"), None, "tensor"),
            P(("groups", "task"), None, "tensor"),
        ),
        check_vma=False,
    )
```

```python
import jax
import jax.numpy as jnp
from jax import lax
from jax.experimental import pallas as pl
from jax.experimental.pallas import tpu as pltpu
from jax.sharding import PartitionSpec as P

ADAPTER_SCALE = 2.0


def block_member(counts, blocks, block_tasks, block_rows):
    tallies = counts.reshape(blocks, block_tasks)
    order = jnp.arange(block_tasks, dtype=jnp.int32)
    upto = order[None, :, None] >= order[None, None, :]
    finish = jnp.sum(jnp.where(upto, tallies[:, None, :], 0), axis=2)
    starts = finish - tallies
    positions = jnp.arange(block_rows, dtype=jnp.int32)
    inside = (positions[None, :, None] >= starts[:, None, :]) & (
        positions[None, :, None] < finish[:, None, :]
    )
    return inside.astype(jnp.float32)


def pack_head(head, n_groups, n_task):
    units, ranks, width = head.shape
    own = width // n_groups
    part = lax.dynamic_slice_in_dim(head, lax.axis_index("groups") * own, own, axis=2)
    part = part.reshape(units, ranks, n_task, own // n_task)
    return part.transpose(2, 0, 1, 3).reshape(n_task, units, -1)


def regroup(packed):
    got = lax.all_to_all(packed, "task", split_axis=0, concat_axis=0, tiled=True)
    return got.reshape(-1, got.shape[2])


def produce(every_hidden, matrix, n_owners):
    made = jnp.dot(every_hidden, matrix, preferred_element_type=jnp.float32)
    return made.astype(jnp.bfloat16).reshape(n_owners, -1, matrix.shape[1])


def to_owners(made):
    return lax.all_to_all(
        made, ("groups", "task"), split_axis=0, concat_axis=0, tiled=True
    )


def corner(array):
    return lax.slice(array, (0,) * array.ndim, (1,) * array.ndim)


def unpack_factor(got, ranks):
    owners, tasks, flat = got.shape
    return (
        got.reshape(owners, tasks, ranks, flat // ranks)
        .transpose(1, 2, 0, 3)
        .reshape(tasks, ranks, -1)
    )


def project_kernel(tokens_ref, factors_ref, mask_ref, pick_ref, out_ref):
    owners, _, flat = factors_ref.shape
    own = tokens_ref.shape[1] // owners
    total = None
    for owner in range(owners):
        stacked = jnp.concatenate(
            [factors_ref[owner, :, at : at + own] for at in range(0, flat, own)], axis=0
        )
        made = lax.dot_general(
            tokens_ref[:, owner * own : (owner + 1) * own],
            stacked,
            (((1,), (1,)), ((), ())),
            preferred_element_type=jnp.float32,
        )
        total = made if total is None else total + made
    out_ref[...] = jnp.dot(
        total * mask_ref[...],
        pick_ref[...],
        precision=lax.Precision.HIGHEST,
        preferred_element_type=jnp.float32,
    )


def project_flat(tokens, got, mask, pick):
    rows, width = tokens.shape
    return pl.pallas_call(
        project_kernel,
        out_shape=jax.ShapeDtypeStruct((rows, pick.shape[1]), jnp.float32),
        in_specs=[pl.BlockSpec(memory_space=pltpu.VMEM)] * 4,
        out_specs=pl.BlockSpec(memory_space=pltpu.VMEM),
        compiler_params=pltpu.CompilerParams(vmem_limit_bytes=24 * 2**20),
        cost_estimate=pl.CostEstimate(
            flops=2 * rows * width * mask.shape[1],
            bytes_accessed=2 * (tokens.size + got.size) + 4 * mask.size,
            transcendentals=0,
        ),
    )(tokens, got, mask, pick)


def local(
    tokens,
    task_counts,
    task_embeddings,
    embedding_weight,
    down_factor_head,
    query_up_head,
    value_up_head,
    w_query,
    w_value,
):
    n_groups, n_task = lax.axis_size("groups"), lax.axis_size("task")
    n_owners = n_groups * n_task
    blocks = lax.axis_size("tensor")
    rank = query_up_head.shape[1]
    rows, shard_width = tokens.shape
    block_rows = rows // blocks
    block_tasks = task_counts.shape[0] // blocks

    after = lax.optimization_barrier

    packed_query = pack_head(query_up_head, n_groups, n_task)
    packed_value = pack_head(value_up_head, n_groups, n_task)
    packed_up = jnp.concatenate((packed_query, packed_value), axis=2)
    flat_query = packed_query.shape[2]

    hidden = jax.nn.silu(
        jnp.dot(task_embeddings, embedding_weight, preferred_element_type=jnp.float32)
    ).astype(jnp.bfloat16)
    every_hidden = to_owners(jnp.broadcast_to(hidden, (n_owners, *hidden.shape)))
    packed_up, _ = after((packed_up, corner(every_hidden)))
    every_hidden = every_hidden.reshape(-1, hidden.shape[1])
    up = regroup(packed_up)

    packed0 = pack_head(down_factor_head[:, :rank], n_groups, n_task)
    packed0, every_hidden, up = after((packed0, every_hidden, up))
    down0 = regroup(packed0)

    sums_query = jnp.dot(tokens, w_query, preferred_element_type=jnp.float32)
    sums_value = jnp.dot(tokens, w_value, preferred_element_type=jnp.float32)
    packed1 = pack_head(down_factor_head[:, rank:], n_groups, n_task)
    made_up = produce(every_hidden, up, n_owners)
    packed1, down0, sums_query, sums_value, made_up = after(
        (packed1, down0, sums_query, sums_value, made_up)
    )
    base_query = lax.psum_scatter(sums_query, "tensor", scatter_dimension=0, tiled=True)
    base_value = lax.psum_scatter(sums_value, "tensor", scatter_dimension=0, tiled=True)
    down1 = regroup(packed1)

    made0 = produce(every_hidden, down0, n_owners)
    made_up, made0, _ = after((made_up, made0, corner(down1)))
    got_up = to_owners(made_up)
    made1 = produce(every_hidden, down1, n_owners)
    made0, made1, got_up = after((made0, made1, got_up))
    every_up = lax.all_gather(got_up, "tensor", axis=0, tiled=False)
    got0 = to_owners(made0)
    query_up_factors = unpack_factor(got_up[:, :, :flat_query], rank)
    value_up_factors = unpack_factor(got_up[:, :, flat_query:], rank)
    made1, got0, base_query, base_value, query_up_factors, value_up_factors = after(
        (made1, got0, base_query, base_value, query_up_factors, value_up_factors)
    )
    got1 = to_owners(made1)
    half0 = unpack_factor(got0, rank)
    half1 = unpack_factor(got1, rank)
    down_factors = jnp.concatenate((half0, half1), axis=1)

    member = block_member(task_counts, blocks, block_tasks, block_rows)
    stretches = tokens.reshape(blocks, block_rows, shard_width)

    def project(half):
        made = jnp.einsum(
            "bpd,bmrd->bpmr",
            stretches,
            half.reshape(blocks, block_tasks, rank, shard_width),
            preferred_element_type=jnp.float32,
        )
        return jnp.sum(made * member[..., None], axis=2).reshape(rows, rank)

    if (shard_width // n_owners) % 128 == 0:
        tasks = task_counts.shape[0]
        same = jnp.repeat(jnp.eye(blocks, dtype=jnp.float32), block_tasks, axis=1)
        mask = jnp.tile(member, (1, 1, blocks)) * same[:, None, :]
        mask = jnp.tile(mask.reshape(rows, tasks), (1, rank))
        pick = jnp.repeat(jnp.eye(2 * rank, dtype=jnp.float32), tasks, axis=0)
        sums = project_flat(tokens, got0, mask, pick[: rank * tasks]) + project_flat(
            tokens, got1, mask, pick[rank * tasks :]
        )
    else:
        sums = jnp.concatenate((project(half0), project(half1)), axis=1)
    low_rank = lax.psum_scatter(
        sums,
        "tensor", scatter_dimension=0, tiled=True,
    )
    own_member = lax.dynamic_index_in_dim(
        member, lax.axis_index("tensor"), axis=0, keepdims=False
    )

    own_up = lax.dynamic_slice_in_dim(
        every_up, lax.axis_index("tensor") * block_tasks, block_tasks, axis=2
    )

    def delta(part, factors):
        spread = (own_member[:, :, None] * part[:, None, :]).reshape(block_rows, -1)
        columns = factors.shape[3] // rank
        whole = factors.reshape(-1, block_tasks, rank, columns).transpose(1, 2, 0, 3)
        return jnp.dot(
            spread,
            whole.reshape(block_tasks * rank, -1).astype(jnp.float32),
            precision=lax.Precision.HIGHEST,
        )

    query = base_query + ADAPTER_SCALE * delta(
        low_rank[:, :rank], own_up[..., :flat_query]
    )
    value = base_value + ADAPTER_SCALE * delta(
        low_rank[:, rank:], own_up[..., flat_query:]
    )
    return (
        query.astype(jnp.bfloat16),
        value.astype(jnp.bfloat16),
        down_factors,
        query_up_factors,
        value_up_factors,
    )


def solution(mesh):
    return jax.shard_map(
        local,
        mesh=mesh,
        in_specs=(
            P(("groups", "task"), "tensor"),
            P(("groups", "task")),
            P(("groups", "task"), None),
            P(),
            P("task", None, "tensor"),
            P("task", None, "tensor"),
            P("task", None, "tensor"),
            P("tensor", None),
            P("tensor", None),
        ),
        out_specs=(
            P(("groups", "task", "tensor"), None),
            P(("groups", "task", "tensor"), None),
            P(("groups", "task"), None, "tensor"),
            P(("groups", "task"), None, "tensor"),
            P(("groups", "task"), None, "tensor"),
        ),
        check_vma=False,
    )
```
